256 devices in a mesh: dp: 32 (over x, y, core), tensor: 8 (over z).
Axes of the slice: x: 4, y: 4, z: 8, core: 2. Of those that a mesh axis runs over, the one named last changes fastest.
Arguments:
- hidden: bfloat16 [32768, 28672], P('dp', 'tensor'), may hold values from -6 to 6
- out_grad: bfloat16 [32768, 8192], P('dp', 'tensor'), may hold values from -6 to 6
- lengths: int32 [64], P('dp'), may hold values from 128 to 512, as said below
- hid_kind: int32 [224], P('tensor'), may hold values from 0 to 7
- hid_sign: int32 [224], P('tensor'), may hold values from 0 to 1
- hid_table: bfloat16 [8, 128, 32], replicated, may hold values from -0.03125 to 0.03125
- out_kind: int32 [64], P('tensor'), may hold values from 0 to 7
- out_sign: int32 [64], P('tensor'), may hold values from 0 to 1
- out_table: bfloat16 [8, 128, 32], replicated, may hold values from -0.0625 to 0.0625
- ridge: float32 [1], replicated, may hold values from 256 to 2048
Outputs:
- whitened: float32 [64, 1024], P('dp')
The draws below stay inside these ranges and needn't reach their ends.
Inputs may be any that keep to these rules, and one draw needn't show every extreme that they name: `lengths`: some sequence has exactly 512 tokens.
All inputs are finite; a program needn't handle non-finite values.
Results may differ from the reference program's by a relative error of at most 0.0003.
Values sent between devices are 32-bit elements; how exact they have to be, the bound alone decides.
No kernel may reach another device: no remote copies, remote signals or barrier semaphores. Data moves between devices by JAX's collectives and lax.ppermute only.
A program may use at most 128 MiB of HBM per device.

```python
import math
import jax
import jax.numpy as jnp
from jax import lax

D = 8192
FF = 28672
SK = 32
BLK = 128
KIND = 8
LMAX = 512
FEAT = 1024
SEQS = 64
TOKENS = 32768


def draw_lengths(key, part):
    key = jax.random.fold_in(key, 5)
    first, second = jax.random.split(key)
    drawn = jax.random.randint(first, (SEQS,), LMAX // 4, LMAX + 1)
    where_full = jax.random.randint(second, (), 0, SEQS)
    return jnp.where(jnp.arange(SEQS) == where_full, LMAX, drawn).astype(jnp.int32)


def with_ends(values, own_key, smallest, high):
    dims = values.shape
    place = [jax.random.randint(jax.random.fold_in(own_key, axis), (), 0, dims[axis]) for axis in range(len(dims))]
    values = values.at[tuple(place)].set(smallest)
    longest = dims.index(max(dims))
    place[longest] = (place[longest] + 1) % dims[longest]
    return values.at[tuple(place)].set(high)


def levels(own_key, shape, cuts, low, largest):
    factor_of, own = 1.0, jax.random.fold_in(own_key, 6)
    for dim, blocks in cuts:
        heights = jnp.exp(jax.random.uniform(jax.random.fold_in(own, dim), (blocks,), jnp.float32, low / len(cuts), largest / len(cuts)))
        factor_of = factor_of * jnp.repeat(heights, shape[dim] // blocks).reshape([-1 if axis == dim else 1 for axis in range(len(shape))])
    return factor_of


def bell_draw(rng, extent, scale, most, pieces=(), kind=jnp.bfloat16):
    entries = scale * jax.random.normal(rng, extent, jnp.float32)
    if pieces:
        entries = entries * levels(rng, extent, pieces, -0.22, 0.18)
    return jnp.clip(entries, -most, most).astype(kind)


def setup_inputs(seed: int = 0) -> dict:
    splits = jax.random.split(jax.random.key(seed), 11)
    hidden = bell_draw(splits[0], (TOKENS, FF), 1.0, 6.0, ((0, 32), (1, 8)))
    out_grad = bell_draw(splits[1], (TOKENS, D), 1.0, 6.0, ((0, 32), (1, 8)))
    lengths = draw_lengths(jax.random.fold_in(splits[10], 71), 0)
    hid_kind = with_ends(jax.random.randint(splits[3], (FF // BLK,), 0, KIND), jax.random.fold_in(splits[3], 1), 0, KIND - 1).astype(jnp.int32)
    hid_sign = with_ends(jax.random.randint(splits[4], (FF // BLK,), 0, 2), jax.random.fold_in(splits[4], 1), 0, 1).astype(jnp.int32)
    hid_table = bell_draw(splits[5], (KIND, BLK, SK), FF ** -0.5, 0.03125)
    out_kind = with_ends(jax.random.randint(splits[6], (D // BLK,), 0, KIND), jax.random.fold_in(splits[6], 1), 0, KIND - 1).astype(jnp.int32)
    out_sign = with_ends(jax.random.randint(splits[7], (D // BLK,), 0, 2), jax.random.fold_in(splits[7], 1), 0, 1).astype(jnp.int32)
    out_table = bell_draw(splits[8], (KIND, BLK, SK), D ** -0.5, 0.0625)
    ridge = jnp.clip(jnp.exp(jax.random.uniform(splits[9], (1,), jnp.float32, math.log(256.0), math.log(2048.0))), 256.0, 2048.0)
    return dict(hidden=hidden, out_grad=out_grad, lengths=lengths, hid_kind=hid_kind, hid_sign=hid_sign, hid_table=hid_table, out_kind=out_kind, out_sign=out_sign, out_table=out_table, ridge=ridge)


def sketch_matrix(kinds, signs, table):
    picks = (kinds[:, None] == jnp.arange(table.shape[0], dtype=jnp.int32)[None, :]).astype(jnp.float32)
    picks = picks * (2 * signs - 1).astype(jnp.float32)[:, None]
    blocks = jnp.einsum('jk,kcm->jcm', picks, table.astype(jnp.float32), precision=lax.Precision.HIGHEST)
    return blocks.reshape(-1, table.shape[2]).astype(jnp.bfloat16)

def reference(hidden, out_grad, lengths, hid_kind, hid_sign, hid_table, out_kind, out_sign, out_table, ridge):
    s_in = sketch_matrix(hid_kind, hid_sign, hid_table)
    s_out = sketch_matrix(out_kind, out_sign, out_table)

    def one_seq(index):
        first = (index * LMAX).astype(jnp.int32)
        rows_h = lax.dynamic_slice_in_dim(hidden, first, LMAX, 0)
        rows_g = lax.dynamic_slice_in_dim(out_grad, first, LMAX, 0)
        left = jnp.dot(rows_h.astype(jnp.float32), s_in.astype(jnp.float32), preferred_element_type=jnp.float32)
        right = jnp.dot(rows_g.astype(jnp.float32), s_out.astype(jnp.float32), preferred_element_type=jnp.float32)
        live = (jnp.arange(LMAX, dtype=jnp.int32) < lengths[index]).astype(jnp.float32)
        left = left * live[:, None]
        outer = jnp.dot(left.T, right, precision=lax.Precision.HIGHEST)
        outer = outer * lax.rsqrt(lengths[index].astype(jnp.float32))
        return outer.reshape(FEAT)
    feats = lax.map(one_seq, jnp.arange(SEQS, dtype=jnp.int32))
    gram = jnp.dot(feats.T, feats, precision=lax.Precision.HIGHEST)
    gram = gram + ridge[0] * jnp.eye(FEAT, dtype=jnp.float32)
    lower = jnp.linalg.cholesky(gram)
    solved = jax.scipy.linalg.solve_triangular(lower, feats.T, lower=True)
    return solved.T * jnp.sqrt(jnp.float32(FEAT))
```

```python
import functools

import jax
import jax.numpy as jnp
from jax import lax
from jax.experimental import pallas as pl
from jax.experimental.pallas import tpu as pltpu
from jax.sharding import PartitionSpec as P

F32 = jnp.float32
BF16 = jnp.bfloat16
LANES = 128
SUB = 8
VMEM = pl.BlockSpec(memory_space=pltpu.VMEM)
SMEM = pl.BlockSpec(memory_space=pltpu.SMEM)
HBM = pl.BlockSpec(memory_space=pl.ANY)


def iota(shape, dim):
    return lax.broadcasted_iota(jnp.int32, shape, dim)


def sketch_kernel(
    which, hid_kind, hid_sign, out_kind, out_sign, hid_table, out_table, hidden, out_grad, x,
    hid_buf, out_buf, hid_pad, out_pad, s_in, s_out, hid_sems, out_sems,
):
    chunks, rows, _ = hid_buf.shape
    first = which[0] * (chunks * rows)
    copies = []
    for c in range(chunks):
        here = pl.ds(pl.multiple_of(first + c * rows, rows), rows)
        copies.append(
            (
                pltpu.make_async_copy(hidden.at[here], hid_buf.at[c], hid_sems.at[c]),
                pltpu.make_async_copy(out_grad.at[here], out_buf.at[c], out_sems.at[c]),
            )
        )
    for pair in copies:
        for copy in pair:
            copy.start()
    kinds, depth, width = hid_table.shape
    zero = jnp.zeros((depth, width), BF16)
    for k in range(kinds):
        hid_pad[k] = jnp.concatenate([hid_table[k], zero, zero, zero], axis=1)
        out_pad[k] = jnp.concatenate([zero, out_table[k], zero, zero], axis=1)

    def fill(kind, sign, pad, s):
        for j in range(kind.shape[0]):
            block = pad[kind[j]]
            s[pl.ds(j * depth, depth), :] = jnp.where(sign[j] > 0, block, -block)

    fill(hid_kind, hid_sign, hid_pad, s_in)
    fill(out_kind, out_sign, out_pad, s_out)
    for c in range(chunks):
        for copy in copies[c]:
            copy.wait()
        part = jnp.dot(hid_buf[c], s_in[...], preferred_element_type=F32)
        part += jnp.dot(out_buf[c], s_out[...], preferred_element_type=F32)
        if c < chunks // 2:
            x[pl.ds(c * rows, rows), :] = part
        else:
            x[pl.ds((c - chunks // 2) * rows, rows), :] += pltpu.roll(part, 2 * width, 1)


def sketch(which, hidden, out_grad, hid_kind, hid_sign, hid_table, out_kind, out_sign, out_table, length):
    chunks = 4
    rows = length // chunks
    deep, wide = hidden.shape[1], out_grad.shape[1]
    return pl.pallas_call(
        sketch_kernel,
        out_shape=jax.ShapeDtypeStruct((length // 2, LANES), F32),
        in_specs=[SMEM] * 5 + [VMEM] * 2 + [HBM] * 2,
        out_specs=VMEM,
        scratch_shapes=[
            pltpu.VMEM((chunks, rows, deep), BF16),
            pltpu.VMEM((chunks, rows, wide), BF16),
            pltpu.VMEM(hid_table.shape[:2] + (LANES,), BF16),
            pltpu.VMEM(out_table.shape[:2] + (LANES,), BF16),
            pltpu.VMEM((deep, LANES), BF16),
            pltpu.VMEM((wide, LANES), BF16),
            pltpu.SemaphoreType.DMA((chunks,)),
            pltpu.SemaphoreType.DMA((chunks,)),
        ],
        compiler_params=pltpu.CompilerParams(vmem_limit_bytes=24 * 2**20),
        name="sketch",
    )(which, hid_kind, hid_sign, out_kind, out_sign, hid_table, out_table, hidden, out_grad)


def outer_kernel(which, lengths, x_ref, other, feats):
    x = x_ref[...] + other[...]
    half = x.shape[0]
    count = lengths[which[0]]
    lane = iota(x.shape, 1)
    place = iota(x.shape, 0) + jnp.where(lane >= LANES // 2, half, 0)
    live = jnp.where(place < count, x, 0.0)
    z = lax.dot_general(
        live, x, (((0,), (0,)), ((), ())), precision=lax.Precision.HIGHEST, preferred_element_type=F32
    )
    row, column = iota((LANES, LANES), 0), iota((LANES, LANES), 1)
    spread = (row == column // 4).astype(F32)
    spread_later = (row - LANES // 2 == column // 4).astype(F32)
    quarter = LANES // 4
    y = jnp.dot(
        z[quarter : 2 * quarter], spread, precision=lax.Precision.HIGHEST, preferred_element_type=F32
    ) + jnp.dot(
        z[3 * quarter :], spread_later, precision=lax.Precision.HIGHEST, preferred_element_type=F32
    )
    own = iota((SUB, LANES), 1) % 4
    total = jnp.zeros((SUB, LANES), F32)
    for q in range(4):
        total += jnp.where(own == q, y[q * SUB : (q + 1) * SUB], 0.0)
    feats[...] = total * lax.rsqrt(jnp.full((SUB, LANES), count, jnp.int32).astype(F32))


def outer(which, lengths, x, other):
    return pl.pallas_call(
        outer_kernel,
        out_shape=jax.ShapeDtypeStruct((SUB, LANES), F32),
        in_specs=[SMEM, SMEM, VMEM, VMEM],
        out_specs=VMEM,
        name="outer",
    )(which, lengths, x, other)


def split(x, parts):
    out = []
    for _ in range(parts):
        piece = x.astype(BF16)
        out.append(piece)
        x = x - piece.astype(F32)
    return out


def whiten_kernel(place, ridge, gathered, out, aug, across, prods):
    seqs = 2 * gathered.shape[0]
    groups = seqs // SUB
    last = gathered.shape[0] - 1
    own = place[0]
    r = ridge[0]
    for g in range(gathered.shape[0]):
        src = gathered[g]
        aug[2 * g, seqs : seqs + SUB, :] = src[:SUB]
        aug[2 * g + 1, seqs : seqs + SUB, :] = src[SUB:]
    mine, tail = gathered[own], gathered[last]
    for h in range(2):
        aug[2 * own + h, seqs : seqs + SUB, :] = tail[h * SUB : (h + 1) * SUB]
        aug[2 * last + h, seqs : seqs + SUB, :] = mine[h * SUB : (h + 1) * SUB]
    for f in range(SUB):
        for i in range(seqs):
            across[f, i : i + 1, :] = aug[i, seqs + f : seqs + f + 1, :]
    for f in range(SUB):
        aug[seqs + f, seqs : seqs + SUB, :] = jnp.zeros((SUB, LANES), F32)

    def products(i8, _):
        def inner(j8, _):
            for ii in range(SUB):
                i = i8 * SUB + ii
                acc = jnp.zeros((SUB, LANES), F32)
                for f in range(SUB):
                    acc += aug[i, pl.ds(seqs + f, 1), :] * across[f, pl.ds(pl.multiple_of(j8 * SUB, SUB), SUB), :]
                prods[i, pl.ds(pl.multiple_of(j8 * SUB, SUB), SUB), :] = acc
            return 0

        return lax.fori_loop(i8, groups, inner, 0)

    lax.fori_loop(0, groups, products, 0)
    before = (iota((LANES, LANES), 0) < iota((LANES, LANES), 1)).astype(BF16)
    for i8 in range(groups):
        wide = seqs - i8 * SUB
        block = prods[i8 * SUB : (i8 + 1) * SUB, i8 * SUB : seqs, :].reshape(SUB * wide, LANES)
        total = sum(jnp.dot(piece, before, preferred_element_type=F32) for piece in split(block, 3))
        aug[i8 * SUB : (i8 + 1) * SUB, i8 * SUB : seqs, :] = total.reshape(SUB, wide, LANES)
    sub = iota((SUB, LANES), 0)
    for i8 in range(groups):
        for ii in range(SUB):
            i = i8 * SUB + ii
            aug[i, i8 * SUB : (i8 + 1) * SUB, :] += jnp.where(sub == ii, r, 0.0)

    for p in range(groups):
        base = p * SUB
        diag = [aug[base + k, base : base + SUB, :] for k in range(SUB)]
        inv = []
        for k in range(SUB):
            inv.append(lax.rsqrt(diag[k][k : k + 1]))
            diag[k] = diag[k] * inv[k]
            for i in range(k + 1, SUB):
                diag[i] = diag[i] - diag[k][i : i + 1] * diag[k]
        for k in range(SUB):
            aug[base + k, base : base + SUB, :] = diag[k]
        for j8 in range(p + 1, groups + 1):
            rows = [aug[base + k, j8 * SUB : (j8 + 1) * SUB, :] for k in range(SUB)]
            for k in range(SUB):
                rows[k] = rows[k] * inv[k]
                for i in range(k + 1, SUB):
                    rows[i] = rows[i] - diag[k][i : i + 1] * rows[k]
            for k in range(SUB):
                aug[base + k, j8 * SUB : (j8 + 1) * SUB, :] = rows[k]

        def trail(i8, _):
            def inner(j8, _):
                cols = pl.ds(pl.multiple_of(j8 * SUB, SUB), SUB)
                rows = [aug[base + k, cols, :] for k in range(SUB)]
                for ii in range(SUB):
                    acc = aug[i8 * SUB + ii, cols, :]
                    for k in range(SUB):
                        acc -= aug[base + k, pl.ds(i8 * SUB + ii, 1), :] * rows[k]
                    aug[i8 * SUB + ii, cols, :] = acc
                return 0

            return lax.fori_loop(i8, groups + 1, inner, 0)

        lax.fori_loop(p + 1, groups + 1, trail, 0)

    end = seqs - 1
    sol_end = aug[end, seqs : seqs + SUB, :] / aug[end, end : end + 1, :]
    sol = (aug[end - 1, seqs : seqs + SUB, :] - aug[end - 1, end : end + 1, :] * sol_end) / aug[
        end - 1, end - 1 : end, :
    ]
    x = [sol * r, sol_end * r]
    schur = [jnp.where(sub == f, r, 0.0) - r * aug[seqs + f, seqs : seqs + SUB, :] for f in range(SUB)]
    w = [jnp.zeros((SUB, LANES), F32) for _ in range(2)]
    for f in range(SUB):
        scale = lax.rsqrt(schur[f][f : f + 1])
        line = schur[f] * scale
        for i in range(f + 1, SUB):
            schur[i] = schur[i] - line[i : i + 1] * line
        for h in range(2):
            value = x[h][f : f + 1] * scale
            w[h] = jnp.where(sub == f, value, w[h])
            x[h] = x[h] - line * value
    size = SUB * LANES
    w = jnp.concatenate(w, axis=0) * jnp.sqrt(jnp.full((2 * SUB, LANES), size, F32))
    spread = (iota((LANES, size), 0) == iota((LANES, size), 1) // SUB).astype(BF16)
    wide = sum(jnp.dot(piece, spread, preferred_element_type=F32) for piece in split(w, 3))
    wide = jnp.where(iota((2 * SUB, size), 1) % SUB == iota((2 * SUB, size), 0) % SUB, wide, 0.0)
    lines = [jnp.sum(wide[h * SUB : (h + 1) * SUB], axis=0, keepdims=True) for h in range(2)]
    swap = place[1] > 0
    out[0:1, :] = jnp.where(swap, lines[1], lines[0])
    out[1:2, :] = jnp.where(swap, lines[0], lines[1])


def whiten(place, ridge, gathered):
    seqs = 2 * gathered.shape[0]
    return pl.pallas_call(
        whiten_kernel,
        out_shape=jax.ShapeDtypeStruct((2, SUB * LANES), F32),
        in_specs=[SMEM, SMEM, VMEM],
        out_specs=VMEM,
        scratch_shapes=[
            pltpu.VMEM((seqs + SUB, seqs + SUB, LANES), F32),
            pltpu.VMEM((SUB, seqs, LANES), F32),
            pltpu.VMEM((seqs, seqs, LANES), F32),
        ],
        compiler_params=pltpu.CompilerParams(vmem_limit_bytes=24 * 2**20),
        name="whiten",
    )(place, ridge, gathered)


def per_device(
    dp, tensor,
    hidden, out_grad, lengths, hid_kind, hid_sign, hid_table, out_kind, out_sign, out_table, ridge
):
    z = lax.axis_index("tensor")
    odd = (z % 2).astype(jnp.int32)
    length = hidden.shape[0] // lengths.shape[0]

    def of(which):
        return sketch(
            which.reshape(1), hidden, out_grad, hid_kind, hid_sign, hid_table, out_kind, out_sign, out_table, length
        )

    def swap(x, bit):
        return lax.ppermute(x, "tensor", [(i, i ^ bit) for i in range(tensor)])

    away = swap(of(1 - odd), 1)
    x = of(odd) + away
    x = x + swap(x, 2)
    feats = outer(odd.reshape(1), lengths, x, swap(x, 4))
    both = jnp.concatenate([feats, swap(feats, 1)], axis=0)
    gathered = lax.all_to_all(jnp.broadcast_to(both[None], (dp,) + both.shape), "dp", 0, 0)
    place = jnp.stack([lax.axis_index("dp").astype(jnp.int32), odd])
    return whiten(place, ridge, gathered)


def solution(mesh):
    return jax.shard_map(
        functools.partial(per_device, mesh.shape["dp"], mesh.shape["tensor"]),
        mesh=mesh,
        in_specs=(
            P("dp", "tensor"),
            P("dp", "tensor"),
            P("dp"),
            P("tensor"),
            P("tensor"),
            P(),
            P("tensor"),
            P("tensor"),
            P(),
            P(),
        ),
        out_specs=P("dp", None),
        check_vma=False,
    )
```

```python
import functools

import jax
import jax.numpy as jnp
from jax import lax
from jax.experimental import pallas as pl
from jax.experimental.pallas import tpu as pltpu
from jax.sharding import PartitionSpec as P

F32 = jnp.float32
BF16 = jnp.bfloat16
LANES = 128
SUB = 8
VMEM = pl.BlockSpec(memory_space=pltpu.VMEM)
SMEM = pl.BlockSpec(memory_space=pltpu.SMEM)
HBM = pl.BlockSpec(memory_space=pl.ANY)


def iota(shape, dim):
    return lax.broadcasted_iota(jnp.int32, shape, dim)


def kept(z):
    return (z + 1) // 2 % 2


def sketch_kernel(
    away, hid_kind, hid_sign, out_kind, out_sign, hid_table, out_table, hidden, out_grad, x,
    hid_buf, out_buf, hid_tab, out_tab, hid_pick, hid_neg, out_pick, out_neg, s_in, s_out, small_sems, hid_sems, out_sem,
):
    which = kept(lax.axis_index("tensor"))
    which = 1 - which if away else which
    chunks, rows, depth = hid_buf.shape
    small = [
        pltpu.make_async_copy(src, dst, small_sems.at[n])
        for n, (src, dst) in enumerate(
            [
                (out_kind, out_pick),
                (out_sign, out_neg),
                (hid_kind, hid_pick),
                (hid_sign, hid_neg),
                (out_table, out_tab),
                (hid_table, hid_tab),
            ]
        )
    ]
    for copy in small:
        copy.start()
    here = pl.ds(pl.multiple_of(which * rows, rows), rows)
    out_copy = pltpu.make_async_copy(out_grad.at[here], out_buf, out_sem)
    out_copy.start()
    hid_copies = [
        pltpu.make_async_copy(hidden.at[here, pl.ds(c * depth, depth)], hid_buf.at[c], hid_sems.at[c])
        for c in range(chunks)
    ]
    for copy in hid_copies:
        copy.start()
    _, width, size = hid_tab.shape
    s_in[...] = jnp.zeros_like(s_in)
    s_out[...] = jnp.zeros_like(s_out)
    for copy in small:
        copy.wait()

    def fill(pick, neg, tab, s, row):
        for j in range(pick.shape[0]):
            block = tab[pick[j]]
            s[row : row + width, j * size : (j + 1) * size] = jnp.where(neg[j] > 0, block, -block)

    fill(out_pick, out_neg, out_tab, s_out, width)
    fill(hid_pick, hid_neg, hid_tab, s_in, 0)

    def times(left, right):
        return lax.dot_general(left, right, (((1,), (1,)), ((), ())), preferred_element_type=F32)

    out_copy.wait()
    total = times(out_buf[...], s_out[...])
    for c in range(chunks):
        hid_copies[c].wait()
        total += times(hid_buf[c], s_in[:, c * depth : (c + 1) * depth])
    half = rows // 2
    x[...] = total[:half] + pltpu.roll(total[half:], 2 * width, 1)


def sketch(away, hidden, out_grad, hid_kind, hid_sign, hid_table, out_kind, out_sign, out_table, length):
    deep, wide = hidden.shape[1], out_grad.shape[1]
    chunks = 7
    return pl.pallas_call(
        functools.partial(sketch_kernel, away),
        out_shape=jax.ShapeDtypeStruct((length // 2, LANES), F32),
        in_specs=[HBM] * 8,
        out_specs=VMEM,
        scratch_shapes=[
            pltpu.VMEM((chunks, length, deep // chunks), BF16),
            pltpu.VMEM((length, wide), BF16),
            pltpu.VMEM(hid_table.shape, BF16),
            pltpu.VMEM(out_table.shape, BF16),
            pltpu.SMEM(hid_kind.shape, jnp.int32),
            pltpu.SMEM(hid_sign.shape, jnp.int32),
            pltpu.SMEM(out_kind.shape, jnp.int32),
            pltpu.SMEM(out_sign.shape, jnp.int32),
            pltpu.VMEM((LANES, deep), BF16),
            pltpu.VMEM((LANES, wide), BF16),
            pltpu.SemaphoreType.DMA((6,)),
            pltpu.SemaphoreType.DMA((chunks,)),
            pltpu.SemaphoreType.DMA,
        ],
        compiler_params=pltpu.CompilerParams(vmem_limit_bytes=24 * 2**20),
        name="sketch_away" if away else "sketch_own",
    )(hid_kind, hid_sign, out_kind, out_sign, hid_table, out_table, hidden, out_grad)


def outer_kernel(lengths, x_ref, other, feats, counts, sem):
    copy = pltpu.make_async_copy(lengths, counts, sem)
    copy.start()
    x = x_ref[...] + other[...]
    half = x.shape[0]
    copy.wait()
    count = counts[kept(lax.axis_index("tensor"))]
    lane = iota(x.shape, 1)
    place = iota(x.shape, 0) + jnp.where(lane >= LANES // 2, half, 0)
    live = jnp.where(place < count, x, 0.0)
    z = lax.dot_general(
        live, x, (((0,), (0,)), ((), ())), precision=lax.Precision.HIGHEST, preferred_element_type=F32
    )
    row, column = iota((LANES, LANES), 0), iota((LANES, LANES), 1)
    spread = (row == column // 4).astype(F32)
    spread_later = (row - LANES // 2 == column // 4).astype(F32)
    quarter = LANES // 4
    y = jnp.dot(
        z[quarter : 2 * quarter], spread, precision=lax.Precision.HIGHEST, preferred_element_type=F32
    ) + jnp.dot(
        z[3 * quarter :], spread_later, precision=lax.Precision.HIGHEST, preferred_element_type=F32
    )
    own = iota((SUB, LANES), 1) % 4
    total = jnp.zeros((SUB, LANES), F32)
    for q in range(4):
        total += jnp.where(own == q, y[q * SUB : (q + 1) * SUB], 0.0)
    feats[...] = total * lax.rsqrt(jnp.full((SUB, LANES), count, jnp.int32).astype(F32))


def outer(lengths, x, other):
    return pl.pallas_call(
        outer_kernel,
        out_shape=jax.ShapeDtypeStruct((SUB, LANES), F32),
        in_specs=[HBM, VMEM, VMEM],
        out_specs=VMEM,
        scratch_shapes=[pltpu.SMEM(lengths.shape, jnp.int32), pltpu.SemaphoreType.DMA],
        name="outer",
    )(lengths, x, other)


def split(x, parts):
    out = []
    for _ in range(parts):
        piece = x.astype(BF16)
        out.append(piece)
        x = x - piece.astype(F32)
    return out


def whiten_kernel(ridge, gathered, out, aug, across, prods, ridge_here, sem):
    copy = pltpu.make_async_copy(ridge, ridge_here, sem)
    copy.start()
    seqs = gathered.shape[0]
    groups = seqs // SUB
    last = seqs // 2 - 1
    own = lax.axis_index("dp")
    for i in range(seqs):
        aug[i, seqs : seqs + SUB, :] = gathered[i]
    for h in range(2):
        aug[2 * own + h, seqs : seqs + SUB, :] = gathered[2 * last + h]
        aug[2 * last + h, seqs : seqs + SUB, :] = gathered[2 * own + h]
    for f in range(SUB):
        for j8 in range(groups):
            across[f, j8 * SUB : (j8 + 1) * SUB, :] = jnp.concatenate([aug[j8 * SUB + i, seqs + f : seqs + f + 1, :] for i in range(SUB)], axis=0)
    for f in range(SUB):
        aug[seqs + f, seqs : seqs + SUB, :] = jnp.zeros((SUB, LANES), F32)

    for i8 in range(groups):
        for i0 in range(0, SUB, 4):
            heads = [
                [jnp.broadcast_to(aug[i8 * SUB + ii, seqs + f : seqs + f + 1, :], (SUB, LANES)) for f in range(SUB)]
                for ii in range(i0, i0 + 4)
            ]
            for j8 in range(i8, groups):
                rows = [across[f, j8 * SUB : (j8 + 1) * SUB, :] for f in range(SUB)]
                for ii in range(4):
                    t = [heads[ii][f] * rows[f] for f in range(SUB)]
                    prods[i8 * SUB + i0 + ii, j8 * SUB : (j8 + 1) * SUB, :] = ((t[0] + t[1]) + (t[2] + t[3])) + (
                        (t[4] + t[5]) + (t[6] + t[7])
                    )
    before = (iota((LANES, LANES), 0) < iota((LANES, LANES), 1)).astype(BF16)
    for i8 in range(groups):
        wide = seqs - i8 * SUB
        block = prods[i8 * SUB : (i8 + 1) * SUB, i8 * SUB : seqs, :].reshape(SUB * wide, LANES)
        total = sum(jnp.dot(piece, before, preferred_element_type=F32) for piece in split(block, 3))
        aug[i8 * SUB : (i8 + 1) * SUB, i8 * SUB : seqs, :] = total.reshape(SUB, wide, LANES)
    copy.wait()
    r = ridge_here[0]
    sub = iota((SUB, LANES), 0)
    for i8 in range(groups):
        for ii in range(SUB):
            i = i8 * SUB + ii
            aug[i, i8 * SUB : (i8 + 1) * SUB, :] += jnp.where(sub == ii, r, 0.0)

    for p in range(groups):
        base = p * SUB
        diag = [aug[base + k, base : base + SUB, :] for k in range(SUB)]
        inv = []
        for k in range(SUB):
            inv.append(lax.rsqrt(diag[k][k : k + 1]))
            diag[k] = diag[k] * inv[k]
            for i in range(k + 1, SUB):
                diag[i] = diag[i] - diag[k][i : i + 1] * diag[k]
        for k in range(SUB):
            aug[base + k, base : base + SUB, :] = diag[k]
        for j8 in range(p + 1, groups + 1):
            rows = [aug[base + k, j8 * SUB : (j8 + 1) * SUB, :] for k in range(SUB)]
            for k in range(SUB):
                rows[k] = rows[k] * inv[k]
                for i in range(k + 1, SUB):
                    rows[i] = rows[i] - diag[k][i : i + 1] * rows[k]
            for k in range(SUB):
                aug[base + k, j8 * SUB : (j8 + 1) * SUB, :] = rows[k]

        for i8 in range(p + 1, groups + 1):
            for i0 in range(0, SUB, 4):
                heads = [
                    [jnp.broadcast_to(aug[base + k, i8 * SUB + ii : i8 * SUB + ii + 1, :], (SUB, LANES)) for k in range(SUB)]
                    for ii in range(i0, i0 + 4)
                ]
                for j8 in range(i8, groups + 1):
                    rows = [aug[base + k, j8 * SUB : (j8 + 1) * SUB, :] for k in range(SUB)]
                    for ii in range(4):
                        h = heads[ii]
                        i = i8 * SUB + i0 + ii
                        acc = aug[i, j8 * SUB : (j8 + 1) * SUB, :]
                        if 1:
                            t = [h[k] * rows[k] for k in range(SUB)]
                            acc = acc - (((t[0] + t[1]) + (t[2] + t[3])) + ((t[4] + t[5]) + (t[6] + t[7])))
                        else:
                            for k in range(SUB):
                                acc = acc - h[k] * rows[k]
                        aug[i, j8 * SUB : (j8 + 1) * SUB, :] = acc

    end = seqs - 1
    sol_end = aug[end, seqs : seqs + SUB, :] / aug[end, end : end + 1, :]
    sol = (aug[end - 1, seqs : seqs + SUB, :] - aug[end - 1, end : end + 1, :] * sol_end) / aug[
        end - 1, end - 1 : end, :
    ]
    x = [sol * r, sol_end * r]
    schur = [jnp.where(sub == f, r, 0.0) - r * aug[seqs + f, seqs : seqs + SUB, :] for f in range(SUB)]
    w = [jnp.zeros((SUB, LANES), F32) for _ in range(2)]
    for f in range(SUB):
        scale = lax.rsqrt(schur[f][f : f + 1])
        line = schur[f] * scale
        for i in range(f + 1, SUB):
            schur[i] = schur[i] - line[i : i + 1] * line
        for h in range(2):
            value = x[h][f : f + 1] * scale
            w[h] = jnp.where(sub == f, value, w[h])
            x[h] = x[h] - line * value
    size = SUB * LANES
    w = jnp.concatenate(w, axis=0) * jnp.sqrt(jnp.full((2 * SUB, LANES), size, F32))
    spread = (iota((LANES, size), 0) == iota((LANES, size), 1) // SUB).astype(BF16)
    wide = sum(jnp.dot(piece, spread, preferred_element_type=F32) for piece in split(w, 3))
    wide = jnp.where(iota((2 * SUB, size), 1) % SUB == iota((2 * SUB, size), 0) % SUB, wide, 0.0)
    lines = [jnp.sum(wide[h * SUB : (h + 1) * SUB], axis=0, keepdims=True) for h in range(2)]
    swap = kept(lax.axis_index("tensor") // 2 * 2) > 0
    out[0:1, :] = jnp.where(swap, lines[1], lines[0])
    out[1:2, :] = jnp.where(swap, lines[0], lines[1])


def whiten(ridge, gathered):
    seqs = gathered.shape[0]
    return pl.pallas_call(
        whiten_kernel,
        out_shape=jax.ShapeDtypeStruct((2, SUB * LANES), F32),
        in_specs=[HBM, VMEM],
        out_specs=VMEM,
        scratch_shapes=[
            pltpu.VMEM((seqs + SUB, seqs + SUB, LANES), F32),
            pltpu.VMEM((SUB, seqs, LANES), F32),
            pltpu.VMEM((seqs, seqs, LANES), F32),
            pltpu.SMEM(ridge.shape, F32),
            pltpu.SemaphoreType.DMA,
        ],
        compiler_params=pltpu.CompilerParams(vmem_limit_bytes=24 * 2**20),
        name="whiten",
    )(ridge, gathered)


def per_device(
    dp, tensor,
    hidden, out_grad, lengths, hid_kind, hid_sign, hid_table, out_kind, out_sign, out_table, ridge
):
    length = hidden.shape[0] // lengths.shape[0]

    def of(away):
        return sketch(
            away, hidden, out_grad, hid_kind, hid_sign, hid_table.swapaxes(1, 2),
            out_kind, out_sign, out_table.swapaxes(1, 2), length,
        )

    def swap(x, other):
        return lax.ppermute(x, "tensor", [(i, other(i) % tensor) for i in range(tensor)])

    x = of(True)
    x = of(False) + swap(x, lambda i: i ^ 1)
    x = x + swap(x, lambda i: i + 1 if i % 2 else i - 1)
    feats = outer(lengths, x, swap(x, lambda i: i - 3 if i % 2 else i + 3))
    groups = [[d * tensor + z + h for d in range(dp) for h in range(2)] for z in range(0, tensor, 2)]
    sent = jnp.broadcast_to(feats[None], (2 * dp,) + feats.shape)
    gathered = lax.all_to_all(sent, ("dp", "tensor"), 0, 0, axis_index_groups=groups)
    return whiten(ridge, gathered)


def solution(mesh):
    return jax.shard_map(
        functools.partial(per_device, mesh.shape["dp"], mesh.shape["tensor"]),
        mesh=mesh,
        in_specs=(
            P("dp", "tensor"),
            P("dp", "tensor"),
            P("dp"),
            P("tensor"),
            P("tensor"),
            P(),
            P("tensor"),
            P("tensor"),
            P(),
            P(),
        ),
        out_specs=P("dp", None),
        check_vma=False,
    )
```

```python
import functools

import jax
import jax.numpy as jnp
from jax import lax
from jax.experimental import pallas as pl
from jax.experimental.pallas import tpu as pltpu
from jax.sharding import PartitionSpec as P

F32 = jnp.float32
BF16 = jnp.bfloat16
LANES = 128
SUB = 8
VMEM = pl.BlockSpec(memory_space=pltpu.VMEM)
SMEM = pl.BlockSpec(memory_space=pltpu.SMEM)
HBM = pl.BlockSpec(memory_space=pltpu.HBM)


def iota(shape, dim):
    return lax.broadcasted_iota(jnp.int32, shape, dim)


def kept(z):
    return (z + 1) // 2 % 2


def sketch_kernel(
    away, hid_kind, hid_sign, out_kind, out_sign, hid_table, out_table, hidden, out_grad, x,
    hid_buf, out_buf, hid_tab, out_tab, hid_pick, hid_neg, out_pick, out_neg, s_in, s_out, small_sems, hid_sems, out_sem,
):
    which = kept(lax.axis_index("tensor"))
    which = 1 - which if away else which
    chunks, rows, depth = hid_buf.shape
    small = [
        pltpu.make_async_copy(src, dst, small_sems.at[n])
        for n, (src, dst) in enumerate(
            [
                (out_kind, out_pick),
                (out_sign, out_neg),
                (hid_kind, hid_pick),
                (hid_sign, hid_neg),
                (out_table, out_tab),
                (hid_table, hid_tab),
            ]
        )
    ]
    for copy in small:
        copy.start()
    here = pl.ds(pl.multiple_of(which * rows, rows), rows)
    out_copy = pltpu.make_async_copy(out_grad.at[here], out_buf, out_sem)
    out_copy.start()
    hid_copies = [
        pltpu.make_async_copy(hidden.at[here, pl.ds(c * depth, depth)], hid_buf.at[c], hid_sems.at[c])
        for c in range(chunks)
    ]
    for copy in hid_copies:
        copy.start()
    _, width, size = hid_tab.shape
    for copy in small:
        copy.wait()

    def fill(pick, neg, tab, s):
        for j in range(pick.shape[0]):
            block = tab[pick[j]]
            s[:, j * size : (j + 1) * size] = jnp.where(neg[j] > 0, block, -block)

    def times(left, right):
        return lax.dot_general(left, right, (((1,), (1,)), ((), ())), preferred_element_type=F32)

    fill(out_pick, out_neg, out_tab, s_out)
    fill(hid_pick, hid_neg, hid_tab, s_in)
    out_copy.wait()
    x[width:, :] = times(s_out[...], out_buf[...])
    total = None
    for c in range(chunks):
        hid_copies[c].wait()
        part = times(s_in[:, c * depth : (c + 1) * depth], hid_buf[c])
        total = part if total is None else total + part
    x[:width, :] = total


def sketch(away, hidden, out_grad, hid_kind, hid_sign, hid_table, out_kind, out_sign, out_table, length):
    deep, wide = hidden.shape[1], out_grad.shape[1]
    chunks = 7
    return pl.pallas_call(
        functools.partial(sketch_kernel, away),
        out_shape=jax.ShapeDtypeStruct((2 * hid_table.shape[1], length), F32),
        in_specs=[HBM] * 8,
        out_specs=VMEM,
        scratch_shapes=[
            pltpu.VMEM((chunks, length, deep // chunks), BF16),
            pltpu.VMEM((length, wide), BF16),
            pltpu.VMEM(hid_table.shape, BF16),
            pltpu.VMEM(out_table.shape, BF16),
            pltpu.SMEM(hid_kind.shape, jnp.int32),
            pltpu.SMEM(hid_sign.shape, jnp.int32),
            pltpu.SMEM(out_kind.shape, jnp.int32),
            pltpu.SMEM(out_sign.shape, jnp.int32),
            pltpu.VMEM((hid_table.shape[1], deep), BF16),
            pltpu.VMEM((out_table.shape[1], wide), BF16),
            pltpu.SemaphoreType.DMA((6,)),
            pltpu.SemaphoreType.DMA((chunks,)),
            pltpu.SemaphoreType.DMA,
        ],
        compiler_params=pltpu.CompilerParams(vmem_limit_bytes=24 * 2**20),
        name="sketch_away" if away else "sketch_own",
    )(*[pltpu.with_memory_space_constraint(v, pltpu.HBM) for v in (hid_kind, hid_sign, out_kind, out_sign, hid_table, out_table, hidden, out_grad)])


def split(x, parts):
    out = []
    for _ in range(parts):
        piece = x.astype(BF16)
        out.append(piece)
        x = x - piece.astype(F32)
    return out


def outer_kernel(lengths, x_ref, other, feats, counts, sem):
    copy = pltpu.make_async_copy(lengths, counts, sem)
    copy.start()
    x = x_ref[...] + other[...]
    width = x.shape[0] // 2
    copy.wait()
    count = counts[kept(lax.axis_index("tensor"))]
    a = jnp.where(iota((width, x.shape[1]), 1) < count, x[:width], 0.0)
    a = jnp.concatenate(split(a, 2), axis=0)
    b = jnp.concatenate(split(x[width:], 2), axis=0)
    z = lax.dot_general(b, a, (((1,), (1,)), ((), ())), preferred_element_type=F32)
    z = z[:width] + z[width:]
    spread = (iota((2 * width, LANES), 0) % width == iota((2 * width, LANES), 1) // 4).astype(BF16)
    y = sum(jnp.dot(piece, spread, preferred_element_type=F32) for piece in split(z, 3))
    own = iota((SUB, LANES), 1) % 4
    total = jnp.zeros((SUB, LANES), F32)
    for q in range(4):
        total += jnp.where(own == q, y[q * SUB : (q + 1) * SUB], 0.0)
    total *= lax.rsqrt(jnp.full((SUB, LANES), count, jnp.int32).astype(F32))
    for n in range(feats.shape[0]):
        feats[n] = total


def outer(lengths, x, other, takers):
    return pl.pallas_call(
        outer_kernel,
        out_shape=jax.ShapeDtypeStruct((takers, SUB, LANES), F32),
        in_specs=[HBM, VMEM, VMEM],
        out_specs=VMEM,
        scratch_shapes=[pltpu.SMEM(lengths.shape, jnp.int32), pltpu.SemaphoreType.DMA],
        name="outer",
    )(lengths, x, other)


def whiten_kernel(ridge, gathered, out, aug, across, prods, ridge_here, sem):
    copy = pltpu.make_async_copy(ridge, ridge_here, sem)
    copy.start()
    seqs = gathered.shape[0]
    groups = seqs // SUB
    last = seqs // 2 - 1
    own = lax.axis_index("dp")
    for i in range(seqs):
        aug[i, seqs : seqs + SUB, :] = gathered[i]
    for h in range(2):
        aug[2 * own + h, seqs : seqs + SUB, :] = gathered[2 * last + h]
        aug[2 * last + h, seqs : seqs + SUB, :] = gathered[2 * own + h]
    for f in range(SUB):
        for j8 in range(groups):
            across[f, j8 * SUB : (j8 + 1) * SUB, :] = jnp.concatenate([aug[j8 * SUB + i, seqs + f : seqs + f + 1, :] for i in range(SUB)], axis=0)
    for f in range(SUB):
        aug[seqs + f, seqs : seqs + SUB, :] = jnp.zeros((SUB, LANES), F32)

    for i8 in range(groups):
        for i0 in range(0, SUB, 4):
            heads = [
                [jnp.broadcast_to(aug[i8 * SUB + ii, seqs + f : seqs + f + 1, :], (SUB, LANES)) for f in range(SUB)]
                for ii in range(i0, i0 + 4)
            ]
            for j8 in range(i8, groups):
                rows = [across[f, j8 * SUB : (j8 + 1) * SUB, :] for f in range(SUB)]
                for ii in range(4):
                    t = [heads[ii][f] * rows[f] for f in range(SUB)]
                    prods[i8 * SUB + i0 + ii, j8 * SUB : (j8 + 1) * SUB, :] = ((t[0] + t[1]) + (t[2] + t[3])) + (
                        (t[4] + t[5]) + (t[6] + t[7])
                    )
    before = (iota((LANES, LANES), 0) < iota((LANES, LANES), 1)).astype(BF16)
    for i8 in range(groups):
        wide = seqs - i8 * SUB
        block = prods[i8 * SUB : (i8 + 1) * SUB, i8 * SUB : seqs, :].reshape(SUB * wide, LANES)
        total = sum(jnp.dot(piece, before, preferred_element_type=F32) for piece in split(block, 3))
        aug[i8 * SUB : (i8 + 1) * SUB, i8 * SUB : seqs, :] = total.reshape(SUB, wide, LANES)
    copy.wait()
    r = ridge_here[0]
    sub = iota((SUB, LANES), 0)
    for i8 in range(groups):
        for ii in range(SUB):
            i = i8 * SUB + ii
            aug[i, i8 * SUB : (i8 + 1) * SUB, :] += jnp.where(sub == ii, r, 0.0)

    for p in range(groups):
        base = p * SUB
        diag = [aug[base + k, base : base + SUB, :] for k in range(SUB)]
        inv = []
        for k in range(SUB):
            inv.append(lax.rsqrt(diag[k][k : k + 1]))
            diag[k] = diag[k] * inv[k]
            for i in range(k + 1, SUB):
                diag[i] = diag[i] - diag[k][i : i + 1] * diag[k]
        for k in range(SUB):
            aug[base + k, base : base + SUB, :] = diag[k]
        for j8 in range(p + 1, groups + 1):
            rows = [aug[base + k, j8 * SUB : (j8 + 1) * SUB, :] for k in range(SUB)]
            for k in range(SUB):
                rows[k] = rows[k] * inv[k]
                for i in range(k + 1, SUB):
                    rows[i] = rows[i] - diag[k][i : i + 1] * rows[k]
            for k in range(SUB):
                aug[base + k, j8 * SUB : (j8 + 1) * SUB, :] = rows[k]

        for i8 in range(p + 1, groups + 1):
            for i0 in range(0, SUB, 4):
                heads = [
                    [jnp.broadcast_to(aug[base + k, i8 * SUB + ii : i8 * SUB + ii + 1, :], (SUB, LANES)) for k in range(SUB)]
                    for ii in range(i0, i0 + 4)
                ]
                for j8 in range(i8, groups + 1):
                    rows = [aug[base + k, j8 * SUB : (j8 + 1) * SUB, :] for k in range(SUB)]
                    for ii in range(4):
                        h = heads[ii]
                        i = i8 * SUB + i0 + ii
                        acc = aug[i, j8 * SUB : (j8 + 1) * SUB, :]
                        if 1:
                            t = [h[k] * rows[k] for k in range(SUB)]
                            acc = acc - (((t[0] + t[1]) + (t[2] + t[3])) + ((t[4] + t[5]) + (t[6] + t[7])))
                        else:
                            for k in range(SUB):
                                acc = acc - h[k] * rows[k]
                        aug[i, j8 * SUB : (j8 + 1) * SUB, :] = acc

    end = seqs - 1
    sol_end = aug[end, seqs : seqs + SUB, :] / aug[end, end : end + 1, :]
    sol = (aug[end - 1, seqs : seqs + SUB, :] - aug[end - 1, end : end + 1, :] * sol_end) / aug[
        end - 1, end - 1 : end, :
    ]
    x = [sol * r, sol_end * r]
    schur = [jnp.where(sub == f, r, 0.0) - r * aug[seqs + f, seqs : seqs + SUB, :] for f in range(SUB)]
    w = [jnp.zeros((SUB, LANES), F32) for _ in range(2)]
    for f in range(SUB):
        scale = lax.rsqrt(schur[f][f : f + 1])
        line = schur[f] * scale
        for i in range(f + 1, SUB):
            schur[i] = schur[i] - line[i : i + 1] * line
        for h in range(2):
            value = x[h][f : f + 1] * scale
            w[h] = jnp.where(sub == f, value, w[h])
            x[h] = x[h] - line * value
    size = SUB * LANES
    w = jnp.concatenate(w, axis=0) * jnp.sqrt(jnp.full((2 * SUB, LANES), size, F32))
    spread = (iota((LANES, size), 0) == iota((LANES, size), 1) // SUB).astype(BF16)
    wide = sum(jnp.dot(piece, spread, preferred_element_type=F32) for piece in split(w, 3))
    wide = jnp.where(iota((2 * SUB, size), 1) % SUB == iota((2 * SUB, size), 0) % SUB, wide, 0.0)
    lines = [jnp.sum(wide[h * SUB : (h + 1) * SUB], axis=0, keepdims=True) for h in range(2)]
    swap = kept(lax.axis_index("tensor") // 2 * 2) > 0
    out[0:1, :] = jnp.where(swap, lines[1], lines[0])
    out[1:2, :] = jnp.where(swap, lines[0], lines[1])


def whiten(ridge, gathered):
    seqs = gathered.shape[0]
    return pl.pallas_call(
        whiten_kernel,
        out_shape=jax.ShapeDtypeStruct((2, SUB * LANES), F32),
        in_specs=[HBM, VMEM],
        out_specs=VMEM,
        scratch_shapes=[
            pltpu.VMEM((seqs + SUB, seqs + SUB, LANES), F32),
            pltpu.VMEM((SUB, seqs, LANES), F32),
            pltpu.VMEM((seqs, seqs, LANES), F32),
            pltpu.SMEM(ridge.shape, F32),
            pltpu.SemaphoreType.DMA,
        ],
        compiler_params=pltpu.CompilerParams(vmem_limit_bytes=24 * 2**20),
        name="whiten",
    )(ridge, gathered)


def per_device(
    dp, tensor,
    hidden, out_grad, lengths, hid_kind, hid_sign, hid_table, out_kind, out_sign, out_table, ridge
):
    length = hidden.shape[0] // lengths.shape[0]

    def of(away):
        return sketch(
            away, hidden, out_grad, hid_kind, hid_sign, hid_table.swapaxes(1, 2),
            out_kind, out_sign, out_table.swapaxes(1, 2), length,
        )

    def swap(x, other):
        return lax.ppermute(x, "tensor", [(i, other(i) % tensor) for i in range(tensor)])

    x = of(True)
    x = of(False) + swap(x, lambda i: i ^ 1)
    x = x + swap(x, lambda i: i + 1 if i % 2 else i - 1)
    feats = outer(lengths, x, swap(x, lambda i: i - 3 if i % 2 else i + 3), 2 * dp)
    groups = [[d * tensor + z + h for d in range(dp) for h in range(2)] for z in range(0, tensor, 2)]
    gathered = lax.all_to_all(feats, ("dp", "tensor"), 0, 0, axis_index_groups=groups)
    return whiten(ridge, gathered)


def solution(mesh):
    return jax.shard_map(
        functools.partial(per_device, mesh.shape["dp"], mesh.shape["tensor"]),
        mesh=mesh,
        in_specs=(
            P("dp", "tensor"),
            P("dp", "tensor"),
            P("dp"),
            P("tensor"),
            P("tensor"),
            P(),
            P("tensor"),
            P("tensor"),
            P(),
            P(),
        ),
        out_specs=P("dp", None),
        check_vma=False,
    )
```

```python
import functools

import jax
import jax.numpy as jnp
from jax import lax
from jax.experimental import pallas as pl
from jax.experimental.pallas import tpu as pltpu
from jax.sharding import PartitionSpec as P

F32 = jnp.float32
BF16 = jnp.bfloat16
LANES = 128
SUB = 8
VMEM = pl.BlockSpec(memory_space=pltpu.VMEM)
SMEM = pl.BlockSpec(memory_space=pltpu.SMEM)
HBM = pl.BlockSpec(memory_space=pltpu.HBM)


def iota(shape, dim):
    return lax.broadcasted_iota(jnp.int32, shape, dim)


def kept(z):
    return (z + 1) // 2 % 2


def sketch_kernel(
    away, lengths, hid_kind, hid_sign, out_kind, out_sign, hid_table, out_table, hidden, out_grad, x,
    hid_buf, out_buf, hid_tab, out_tab, counts, hid_pick, hid_neg, out_pick, out_neg, s_in, s_out, small_sems, hid_sems, out_sem,
):
    which = kept(lax.axis_index("tensor"))
    which = 1 - which if away else which
    chunks, rows, depth = hid_buf.shape
    small = [
        pltpu.make_async_copy(src, dst, small_sems.at[n])
        for n, (src, dst) in enumerate(
            [
                (out_kind, out_pick),
                (out_sign, out_neg),
                (hid_kind, hid_pick),
                (hid_sign, hid_neg),
                (out_table, out_tab),
                (hid_table, hid_tab),
                (lengths, counts),
            ]
        )
    ]
    for copy in small:
        copy.start()
    here = pl.ds(pl.multiple_of(which * rows, rows), rows)
    out_copy = pltpu.make_async_copy(out_grad.at[here], out_buf, out_sem)
    out_copy.start()
    hid_copies = [
        pltpu.make_async_copy(hidden.at[here, pl.ds(c * depth, depth)], hid_buf.at[c], hid_sems.at[c])
        for c in range(chunks)
    ]
    for copy in hid_copies:
        copy.start()
    _, width, size = hid_tab.shape
    for copy in small:
        copy.wait()

    def fill(pick, neg, tab, s):
        for j in range(pick.shape[0]):
            block = tab[pick[j]]
            s[:, j * size : (j + 1) * size] = jnp.where(neg[j] > 0, block, -block)

    def times(left, right):
        return lax.dot_general(left, right, (((1,), (1,)), ((), ())), preferred_element_type=F32)

    fill(out_pick, out_neg, out_tab, s_out)
    fill(hid_pick, hid_neg, hid_tab, s_in)
    out_copy.wait()
    x[width:, :] = times(s_out[...], out_buf[...])
    total = None
    for c in range(chunks):
        hid_copies[c].wait()
        part = times(s_in[:, c * depth : (c + 1) * depth], hid_buf[c])
        total = part if total is None else total + part
    count = counts[which]
    live = iota(total.shape, 1) < count
    scale = lax.rsqrt(jnp.full((1, total.shape[1]), count, jnp.int32).astype(F32))
    x[:width, :] = jnp.where(live, total * scale, 0.0)


def sketch(away, hidden, out_grad, lengths, hid_kind, hid_sign, hid_table, out_kind, out_sign, out_table, length):
    deep, wide = hidden.shape[1], out_grad.shape[1]
    chunks = 7
    operands = (lengths, hid_kind, hid_sign, out_kind, out_sign, hid_table, out_table, hidden, out_grad)
    return pl.pallas_call(
        functools.partial(sketch_kernel, away),
        out_shape=jax.ShapeDtypeStruct((2 * hid_table.shape[1], length), F32),
        in_specs=[HBM] * len(operands),
        out_specs=VMEM,
        scratch_shapes=[
            pltpu.VMEM((chunks, length, deep // chunks), BF16),
            pltpu.VMEM((length, wide), BF16),
            pltpu.VMEM(hid_table.shape, BF16),
            pltpu.VMEM(out_table.shape, BF16),
            pltpu.SMEM(lengths.shape, jnp.int32),
            pltpu.SMEM(hid_kind.shape, jnp.int32),
            pltpu.SMEM(hid_sign.shape, jnp.int32),
            pltpu.SMEM(out_kind.shape, jnp.int32),
            pltpu.SMEM(out_sign.shape, jnp.int32),
            pltpu.VMEM((hid_table.shape[1], deep), BF16),
            pltpu.VMEM((out_table.shape[1], wide), BF16),
            pltpu.SemaphoreType.DMA((7,)),
            pltpu.SemaphoreType.DMA((chunks,)),
            pltpu.SemaphoreType.DMA,
        ],
        compiler_params=pltpu.CompilerParams(vmem_limit_bytes=24 * 2**20),
        name="sketch_away" if away else "sketch_own",
    )(*[pltpu.with_memory_space_constraint(v, pltpu.HBM) for v in operands])


def split(x, parts):
    out = []
    for _ in range(parts):
        piece = x.astype(BF16)
        out.append(piece)
        x = x - piece.astype(F32)
    return out


def outer_kernel(x_ref, other, feats):
    x = x_ref[...] + other[...]
    width = x.shape[0] // 2
    a = jnp.concatenate(split(x[:width], 2), axis=0)
    b = jnp.concatenate(split(x[width:], 2), axis=0)
    z = lax.dot_general(b, a, (((1,), (1,)), ((), ())), preferred_element_type=F32)
    z = z[:width] + z[width:]
    spread = (iota((2 * width, LANES), 0) % width == iota((2 * width, LANES), 1) // 4).astype(BF16)
    y = jnp.dot(jnp.concatenate(split(z, 3), axis=0), spread, preferred_element_type=F32)
    y = y[:width] + y[width : 2 * width] + y[2 * width :]
    own = iota((SUB, LANES), 1) % 4
    total = jnp.zeros((SUB, LANES), F32)
    for q in range(4):
        total += jnp.where(own == q, y[q * SUB : (q + 1) * SUB], 0.0)
    for n in range(feats.shape[0]):
        feats[n] = total


def outer(x, other, takers):
    return pl.pallas_call(
        outer_kernel,
        out_shape=jax.ShapeDtypeStruct((takers, SUB, LANES), F32),
        in_specs=[VMEM, VMEM],
        out_specs=VMEM,
        compiler_params=pltpu.CompilerParams(vmem_limit_bytes=8 * 2**20),
        name="outer",
    )(x, other)


def whiten_kernel(ridge, gathered, out, aug, across, prods, ridge_here, sem):
    copy = pltpu.make_async_copy(ridge, ridge_here, sem)
    copy.start()
    seqs = gathered.shape[0]
    groups = seqs // SUB
    last = seqs // 2 - 1
    own = lax.axis_index("dp")
    for i in range(seqs):
        aug[i, seqs : seqs + SUB, :] = gathered[i]
    for h in range(2):
        aug[2 * own + h, seqs : seqs + SUB, :] = gathered[2 * last + h]
        aug[2 * last + h, seqs : seqs + SUB, :] = gathered[2 * own + h]
    for f in range(SUB):
        for j8 in range(groups):
            across[f, j8 * SUB : (j8 + 1) * SUB, :] = jnp.concatenate([aug[j8 * SUB + i, seqs + f : seqs + f + 1, :] for i in range(SUB)], axis=0)
    for f in range(SUB):
        aug[seqs + f, seqs : seqs + SUB, :] = jnp.zeros((SUB, LANES), F32)

    for i8 in range(groups):
        for i0 in range(0, SUB, 4):
            heads = [
                [jnp.broadcast_to(aug[i8 * SUB + ii, seqs + f : seqs + f + 1, :], (SUB, LANES)) for f in range(SUB)]
                for ii in range(i0, i0 + 4)
            ]
            for j8 in range(i8, groups):
                rows = [across[f, j8 * SUB : (j8 + 1) * SUB, :] for f in range(SUB)]
                for ii in range(4):
                    t = [heads[ii][f] * rows[f] for f in range(SUB)]
                    prods[i8 * SUB + i0 + ii, j8 * SUB : (j8 + 1) * SUB, :] = ((t[0] + t[1]) + (t[2] + t[3])) + (
                        (t[4] + t[5]) + (t[6] + t[7])
                    )
    before = (iota((LANES, LANES), 0) < iota((LANES, LANES), 1)).astype(BF16)
    for i8 in range(groups):
        wide = seqs - i8 * SUB
        block = prods[i8 * SUB : (i8 + 1) * SUB, i8 * SUB : seqs, :].reshape(SUB * wide, LANES)
        total = sum(jnp.dot(piece, before, preferred_element_type=F32) for piece in split(block, 3))
        aug[i8 * SUB : (i8 + 1) * SUB, i8 * SUB : seqs, :] = total.reshape(SUB, wide, LANES)
    copy.wait()
    r = ridge_here[0]
    sub = iota((SUB, LANES), 0)
    for i8 in range(groups):
        for ii in range(SUB):
            i = i8 * SUB + ii
            aug[i, i8 * SUB : (i8 + 1) * SUB, :] += jnp.where(sub == ii, r, 0.0)

    for p in range(groups):
        base = p * SUB
        diag = [aug[base + k, base : base + SUB, :] for k in range(SUB)]
        inv = []
        for k in range(SUB):
            inv.append(lax.rsqrt(diag[k][k : k + 1]))
            diag[k] = diag[k] * inv[k]
            for i in range(k + 1, SUB):
                diag[i] = diag[i] - diag[k][i : i + 1] * diag[k]
        for k in range(SUB):
            aug[base + k, base : base + SUB, :] = diag[k]
        for j8 in range(p + 1, groups + 1):
            rows = [aug[base + k, j8 * SUB : (j8 + 1) * SUB, :] for k in range(SUB)]
            for k in range(SUB):
                rows[k] = rows[k] * inv[k]
                for i in range(k + 1, SUB):
                    rows[i] = rows[i] - diag[k][i : i + 1] * rows[k]
            for k in range(SUB):
                aug[base + k, j8 * SUB : (j8 + 1) * SUB, :] = rows[k]

        for i8 in range(p + 1, groups + 1):
            for i0 in range(0, SUB, 4):
                heads = [
                    [jnp.broadcast_to(aug[base + k, i8 * SUB + ii : i8 * SUB + ii + 1, :], (SUB, LANES)) for k in range(SUB)]
                    for ii in range(i0, i0 + 4)
                ]
                for j8 in range(i8, groups + 1):
                    rows = [aug[base + k, j8 * SUB : (j8 + 1) * SUB, :] for k in range(SUB)]
                    for ii in range(4):
                        h = heads[ii]
                        i = i8 * SUB + i0 + ii
                        acc = aug[i, j8 * SUB : (j8 + 1) * SUB, :]
                        if 1:
                            t = [h[k] * rows[k] for k in range(SUB)]
                            acc = acc - (((t[0] + t[1]) + (t[2] + t[3])) + ((t[4] + t[5]) + (t[6] + t[7])))
                        else:
                            for k in range(SUB):
                                acc = acc - h[k] * rows[k]
                        aug[i, j8 * SUB : (j8 + 1) * SUB, :] = acc

    end = seqs - 1
    sol_end = aug[end, seqs : seqs + SUB, :] / aug[end, end : end + 1, :]
    sol = (aug[end - 1, seqs : seqs + SUB, :] - aug[end - 1, end : end + 1, :] * sol_end) / aug[
        end - 1, end - 1 : end, :
    ]
    x = [sol * r, sol_end * r]
    schur = [jnp.where(sub == f, r, 0.0) - r * aug[seqs + f, seqs : seqs + SUB, :] for f in range(SUB)]
    w = [jnp.zeros((SUB, LANES), F32) for _ in range(2)]
    for f in range(SUB):
        scale = lax.rsqrt(schur[f][f : f + 1])
        line = schur[f] * scale
        for i in range(f + 1, SUB):
            schur[i] = schur[i] - line[i : i + 1] * line
        for h in range(2):
            value = x[h][f : f + 1] * scale
            w[h] = jnp.where(sub == f, value, w[h])
            x[h] = x[h] - line * value
    size = SUB * LANES
    w = jnp.concatenate(w, axis=0) * jnp.sqrt(jnp.full((2 * SUB, LANES), size, F32))
    spread = (iota((LANES, size), 0) == iota((LANES, size), 1) // SUB).astype(BF16)
    wide = sum(jnp.dot(piece, spread, preferred_element_type=F32) for piece in split(w, 3))
    wide = jnp.where(iota((2 * SUB, size), 1) % SUB == iota((2 * SUB, size), 0) % SUB, wide, 0.0)
    lines = [jnp.sum(wide[h * SUB : (h + 1) * SUB], axis=0, keepdims=True) for h in range(2)]
    swap = kept(lax.axis_index("tensor") // 2 * 2) > 0
    out[0:1, :] = jnp.where(swap, lines[1], lines[0])
    out[1:2, :] = jnp.where(swap, lines[0], lines[1])


def whiten(ridge, gathered):
    seqs = gathered.shape[0]
    return pl.pallas_call(
        whiten_kernel,
        out_shape=jax.ShapeDtypeStruct((2, SUB * LANES), F32),
        in_specs=[HBM, VMEM],
        out_specs=VMEM,
        scratch_shapes=[
            pltpu.VMEM((seqs + SUB, seqs + SUB, LANES), F32),
            pltpu.VMEM((SUB, seqs, LANES), F32),
            pltpu.VMEM((seqs, seqs, LANES), F32),
            pltpu.SMEM(ridge.shape, F32),
            pltpu.SemaphoreType.DMA,
        ],
        compiler_params=pltpu.CompilerParams(vmem_limit_bytes=24 * 2**20),
        name="whiten",
    )(ridge, gathered)


def per_device(
    dp, tensor,
    hidden, out_grad, lengths, hid_kind, hid_sign, hid_table, out_kind, out_sign, out_table, ridge
):
    length = hidden.shape[0] // lengths.shape[0]

    def of(away):
        return sketch(
            away, hidden, out_grad, lengths, hid_kind, hid_sign, hid_table.swapaxes(1, 2),
            out_kind, out_sign, out_table.swapaxes(1, 2), length,
        )

    def swap(x, other):
        return lax.ppermute(x, "tensor", [(i, other(i) % tensor) for i in range(tensor)])

    x = of(True)
    x = of(False) + swap(x, lambda i: i ^ 1)
    x = x + swap(x, lambda i: i + 1 if i % 2 else i - 1)
    feats = outer(x, swap(x, lambda i: i - 3 if i % 2 else i + 3), 2 * dp)
    groups = [[d * tensor + z + h for d in range(dp) for h in range(2)] for z in range(0, tensor, 2)]
    gathered = lax.all_to_all(feats, ("dp", "tensor"), 0, 0, axis_index_groups=groups)
    return whiten(ridge, gathered)


def solution(mesh):
    return jax.shard_map(
        functools.partial(per_device, mesh.shape["dp"], mesh.shape["tensor"]),
        mesh=mesh,
        in_specs=(
            P("dp", "tensor"),
            P("dp", "tensor"),
            P("dp"),
            P("tensor"),
            P("tensor"),
            P(),
            P("tensor"),
            P("tensor"),
            P(),
            P(),
        ),
        out_specs=P("dp", None),
        check_vma=False,
    )
```

```python
import functools

import jax
import jax.numpy as jnp
from jax import lax
from jax.experimental import pallas as pl
from jax.experimental.pallas import tpu as pltpu
from jax.sharding import PartitionSpec as P

F32 = jnp.float32
BF16 = jnp.bfloat16
LANES = 128
SUB = 8
VMEM = pl.BlockSpec(memory_space=pltpu.VMEM)
SMEM = pl.BlockSpec(memory_space=pltpu.SMEM)
HBM = pl.BlockSpec(memory_space=pltpu.HBM)


def iota(shape, dim):
    return lax.broadcasted_iota(jnp.int32, shape, dim)


def kept(z):
    return (z + 1) // 2 % 2


def sketch_kernel(
    away, lengths, hid_kind, hid_sign, out_kind, out_sign, hid_table, out_table, hidden, out_grad, x,
    hid_buf, out_buf, hid_tab, out_tab, counts, hid_pick, hid_neg, out_pick, out_neg, s_in, s_out, small_sems, hid_sem, out_sem,
):
    which = kept(lax.axis_index("tensor"))
    which = 1 - which if away else which
    rows, _ = hid_buf.shape
    small = [
        pltpu.make_async_copy(src, dst, small_sems.at[n])
        for n, (src, dst) in enumerate(
            [
                (out_kind, out_pick),
                (out_sign, out_neg),
                (hid_kind, hid_pick),
                (hid_sign, hid_neg),
                (out_table, out_tab),
                (hid_table, hid_tab),
                (lengths, counts),
            ]
        )
    ]
    for copy in small:
        copy.start()
    here = pl.ds(pl.multiple_of(which * rows, rows), rows)
    out_copy = pltpu.make_async_copy(out_grad.at[here], out_buf, out_sem)
    out_copy.start()
    hid_copy = pltpu.make_async_copy(hidden.at[here], hid_buf, hid_sem)
    hid_copy.start()
    _, width, size = hid_tab.shape
    for copy in small:
        copy.wait()

    def fill(pick, neg, tab, s):
        for j in range(pick.shape[0]):
            block = tab[pick[j]]
            s[:, j * size : (j + 1) * size] = jnp.where(neg[j] > 0, block, -block)

    def times(left, right):
        return lax.dot_general(left, right, (((1,), (1,)), ((), ())), preferred_element_type=F32)

    fill(out_pick, out_neg, out_tab, s_out)
    fill(hid_pick, hid_neg, hid_tab, s_in)
    out_copy.wait()
    x[width:, :] = times(s_out[...], out_buf[...])
    hid_copy.wait()
    total = times(s_in[...], hid_buf[...])
    count = counts[which]
    live = iota(total.shape, 1) < count
    scale = lax.rsqrt(jnp.full((1, total.shape[1]), count, jnp.int32).astype(F32))
    x[:width, :] = jnp.where(live, total * scale, 0.0)


def sketch(away, hidden, out_grad, lengths, hid_kind, hid_sign, hid_table, out_kind, out_sign, out_table, length):
    deep, wide = hidden.shape[1], out_grad.shape[1]
    operands = (lengths, hid_kind, hid_sign, out_kind, out_sign, hid_table, out_table, hidden, out_grad)
    return pl.pallas_call(
        functools.partial(sketch_kernel, away),
        out_shape=jax.ShapeDtypeStruct((2 * hid_table.shape[1], length), F32),
        in_specs=[HBM] * len(operands),
        out_specs=VMEM,
        scratch_shapes=[
            pltpu.VMEM((length, deep), BF16),
            pltpu.VMEM((length, wide), BF16),
            pltpu.VMEM(hid_table.shape, BF16),
            pltpu.VMEM(out_table.shape, BF16),
            pltpu.SMEM(lengths.shape, jnp.int32),
            pltpu.SMEM(hid_kind.shape, jnp.int32),
            pltpu.SMEM(hid_sign.shape, jnp.int32),
            pltpu.SMEM(out_kind.shape, jnp.int32),
            pltpu.SMEM(out_sign.shape, jnp.int32),
            pltpu.VMEM((hid_table.shape[1], deep), BF16),
            pltpu.VMEM((out_table.shape[1], wide), BF16),
            pltpu.SemaphoreType.DMA((7,)),
            pltpu.SemaphoreType.DMA,
            pltpu.SemaphoreType.DMA,
        ],
        compiler_params=pltpu.CompilerParams(vmem_limit_bytes=24 * 2**20),
        name="sketch_away" if away else "sketch_own",
    )(*[pltpu.with_memory_space_constraint(v, pltpu.HBM) for v in operands])


def split(x, parts):
    out = []
    for _ in range(parts):
        piece = x.astype(BF16)
        out.append(piece)
        x = x - piece.astype(F32)
    return out


def outer_kernel(x_ref, other, feats):
    x = x_ref[...] + other[...]
    width = x.shape[0] // 2
    a = jnp.concatenate(split(x[:width], 2), axis=0)
    b = jnp.concatenate(split(x[width:], 2), axis=0)
    z = lax.dot_general(b, a, (((1,), (1,)), ((), ())), preferred_element_type=F32)
    z = z[:width] + z[width:]
    spread = (iota((2 * width, LANES), 0) % width == iota((2 * width, LANES), 1) // 4).astype(BF16)
    y = jnp.dot(jnp.concatenate(split(z, 3), axis=0), spread, preferred_element_type=F32)
    y = y[:width] + y[width : 2 * width] + y[2 * width :]
    own = iota((SUB, LANES), 1) % 4
    total = jnp.zeros((SUB, LANES), F32)
    for q in range(4):
        total += jnp.where(own == q, y[q * SUB : (q + 1) * SUB], 0.0)
    for n in range(feats.shape[0]):
        feats[n] = total


def outer(x, other, takers):
    return pl.pallas_call(
        outer_kernel,
        out_shape=jax.ShapeDtypeStruct((takers, SUB, LANES), F32),
        in_specs=[VMEM, VMEM],
        out_specs=VMEM,
        compiler_params=pltpu.CompilerParams(vmem_limit_bytes=8 * 2**20),
        name="outer",
    )(x, other)


def whiten_kernel(ridge, gathered, out, aug, across, prods, ridge_here, sem):
    copy = pltpu.make_async_copy(ridge, ridge_here, sem)
    copy.start()
    seqs = gathered.shape[0]
    groups = seqs // SUB
    last = seqs // 2 - 1
    own = lax.axis_index("dp")
    for i in range(seqs):
        aug[i, seqs : seqs + SUB, :] = gathered[i]
    for h in range(2):
        aug[2 * own + h, seqs : seqs + SUB, :] = gathered[2 * last + h]
        aug[2 * last + h, seqs : seqs + SUB, :] = gathered[2 * own + h]
    for f in range(SUB):
        for j8 in range(groups):
            across[f, j8 * SUB : (j8 + 1) * SUB, :] = jnp.concatenate([aug[j8 * SUB + i, seqs + f : seqs + f + 1, :] for i in range(SUB)], axis=0)
    for f in range(SUB):
        aug[seqs + f, seqs : seqs + SUB, :] = jnp.zeros((SUB, LANES), F32)

    for i8 in range(groups):
        for i0 in range(0, SUB, 4):
            heads = [
                [jnp.broadcast_to(aug[i8 * SUB + ii, seqs + f : seqs + f + 1, :], (SUB, LANES)) for f in range(SUB)]
                for ii in range(i0, i0 + 4)
            ]
            for j8 in range(i8, groups):
                rows = [across[f, j8 * SUB : (j8 + 1) * SUB, :] for f in range(SUB)]
                for ii in range(4):
                    t = [heads[ii][f] * rows[f] for f in range(SUB)]
                    prods[i8 * SUB + i0 + ii, j8 * SUB : (j8 + 1) * SUB, :] = ((t[0] + t[1]) + (t[2] + t[3])) + (
                        (t[4] + t[5]) + (t[6] + t[7])
                    )
    before = (iota((LANES, LANES), 0) < iota((LANES, LANES), 1)).astype(BF16)
    for i8 in range(groups):
        wide = seqs - i8 * SUB
        block = prods[i8 * SUB : (i8 + 1) * SUB, i8 * SUB : seqs, :].reshape(SUB * wide, LANES)
        total = sum(jnp.dot(piece, before, preferred_element_type=F32) for piece in split(block, 2))
        aug[i8 * SUB : (i8 + 1) * SUB, i8 * SUB : seqs, :] = total.reshape(SUB, wide, LANES)
    copy.wait()
    r = ridge_here[0]
    sub = iota((SUB, LANES), 0)
    for i8 in range(groups):
        for ii in range(SUB):
            i = i8 * SUB + ii
            aug[i, i8 * SUB : (i8 + 1) * SUB, :] += jnp.where(sub == ii, r, 0.0)

    for p in range(groups):
        base = p * SUB
        diag = [aug[base + k, base : base + SUB, :] for k in range(SUB)]
        inv = []
        for k in range(SUB):
            inv.append(lax.rsqrt(diag[k][k : k + 1]))
            diag[k] = diag[k] * inv[k]
            for i in range(k + 1, SUB):
                diag[i] = diag[i] - diag[k][i : i + 1] * diag[k]
        for k in range(SUB):
            aug[base + k, base : base + SUB, :] = diag[k]
        for j8 in range(p + 1, groups + 1):
            rows = [aug[base + k, j8 * SUB : (j8 + 1) * SUB, :] for k in range(SUB)]
            for k in range(SUB):
                rows[k] = rows[k] * inv[k]
                for i in range(k + 1, SUB):
                    rows[i] = rows[i] - diag[k][i : i + 1] * rows[k]
            for k in range(SUB):
                aug[base + k, j8 * SUB : (j8 + 1) * SUB, :] = rows[k]

        for i8 in range(p + 1, groups + 1):
            for i0 in range(0, SUB, 4):
                heads = [
                    [jnp.broadcast_to(aug[base + k, i8 * SUB + ii : i8 * SUB + ii + 1, :], (SUB, LANES)) for k in range(SUB)]
                    for ii in range(i0, i0 + 4)
                ]
                for j8 in range(i8, groups + 1):
                    rows = [aug[base + k, j8 * SUB : (j8 + 1) * SUB, :] for k in range(SUB)]
                    for ii in range(4):
                        h = heads[ii]
                        i = i8 * SUB + i0 + ii
                        acc = aug[i, j8 * SUB : (j8 + 1) * SUB, :]
                        if 1:
                            t = [h[k] * rows[k] for k in range(SUB)]
                            acc = acc - (((t[0] + t[1]) + (t[2] + t[3])) + ((t[4] + t[5]) + (t[6] + t[7])))
                        else:
                            for k in range(SUB):
                                acc = acc - h[k] * rows[k]
                        aug[i, j8 * SUB : (j8 + 1) * SUB, :] = acc

    end = seqs - 1
    sol_end = aug[end, seqs : seqs + SUB, :] / aug[end, end : end + 1, :]
    sol = (aug[end - 1, seqs : seqs + SUB, :] - aug[end - 1, end : end + 1, :] * sol_end) / aug[
        end - 1, end - 1 : end, :
    ]
    x = [sol * r, sol_end * r]
    schur = [jnp.where(sub == f, r, 0.0) - r * aug[seqs + f, seqs : seqs + SUB, :] for f in range(SUB)]
    w = [jnp.zeros((SUB, LANES), F32) for _ in range(2)]
    for f in range(SUB):
        scale = lax.rsqrt(schur[f][f : f + 1])
        line = schur[f] * scale
        for i in range(f + 1, SUB):
            schur[i] = schur[i] - line[i : i + 1] * line
        for h in range(2):
            value = x[h][f : f + 1] * scale
            w[h] = jnp.where(sub == f, value, w[h])
            x[h] = x[h] - line * value
    size = SUB * LANES
    w = jnp.concatenate(w, axis=0) * jnp.sqrt(jnp.full((2 * SUB, LANES), size, F32))
    spread = (iota((LANES, size), 0) == iota((LANES, size), 1) // SUB).astype(BF16)
    wide = sum(jnp.dot(piece, spread, preferred_element_type=F32) for piece in split(w, 3))
    wide = jnp.where(iota((2 * SUB, size), 1) % SUB == iota((2 * SUB, size), 0) % SUB, wide, 0.0)
    lines = [jnp.sum(wide[h * SUB : (h + 1) * SUB], axis=0, keepdims=True) for h in range(2)]
    swap = kept(lax.axis_index("tensor") // 2 * 2) > 0
    out[0:1, :] = jnp.where(swap, lines[1], lines[0])
    out[1:2, :] = jnp.where(swap, lines[0], lines[1])


def whiten(ridge, gathered):
    seqs = gathered.shape[0]
    return pl.pallas_call(
        whiten_kernel,
        out_shape=jax.ShapeDtypeStruct((2, SUB * LANES), F32),
        in_specs=[HBM, VMEM],
        out_specs=VMEM,
        scratch_shapes=[
            pltpu.VMEM((seqs + SUB, seqs + SUB, LANES), F32),
            pltpu.VMEM((SUB, seqs, LANES), F32),
            pltpu.VMEM((seqs, seqs, LANES), F32),
            pltpu.SMEM(ridge.shape, F32),
            pltpu.SemaphoreType.DMA,
        ],
        compiler_params=pltpu.CompilerParams(vmem_limit_bytes=24 * 2**20),
        name="whiten",
    )(ridge, gathered)


def per_device(
    dp, tensor,
    hidden, out_grad, lengths, hid_kind, hid_sign, hid_table, out_kind, out_sign, out_table, ridge
):
    length = hidden.shape[0] // lengths.shape[0]

    def of(away):
        return sketch(
            away, hidden, out_grad, lengths, hid_kind, hid_sign, hid_table.swapaxes(1, 2),
            out_kind, out_sign, out_table.swapaxes(1, 2), length,
        )

    def swap(x, other):
        return lax.ppermute(x, "tensor", [(i, other(i) % tensor) for i in range(tensor)])

    x = of(True)
    x = of(False) + swap(x, lambda i: i ^ 1)
    x = x + swap(x, lambda i: i + 1 if i % 2 else i - 1)
    feats = outer(x, swap(x, lambda i: i - 3 if i % 2 else i + 3), 2 * dp)
    groups = [[d * tensor + z + h for d in range(dp) for h in range(2)] for z in range(0, tensor, 2)]
    gathered = lax.all_to_all(feats, ("dp", "tensor"), 0, 0, axis_index_groups=groups)
    return whiten(ridge, gathered)


def solution(mesh):
    return jax.shard_map(
        functools.partial(per_device, mesh.shape["dp"], mesh.shape["tensor"]),
        mesh=mesh,
        in_specs=(
            P("dp", "tensor"),
            P("dp", "tensor"),
            P("dp"),
            P("tensor"),
            P("tensor"),
            P(),
            P("tensor"),
            P("tensor"),
            P(),
            P(),
        ),
        out_specs=P("dp", None),
        check_vma=False,
    )
```

```python
import functools

import jax
import jax.numpy as jnp
from jax import lax
from jax.experimental import pallas as pl
from jax.experimental.pallas import tpu as pltpu
from jax.sharding import PartitionSpec as P

F32 = jnp.float32
BF16 = jnp.bfloat16
LANES = 128
SUB = 8
VMEM = pl.BlockSpec(memory_space=pltpu.VMEM)
SMEM = pl.BlockSpec(memory_space=pltpu.SMEM)
HBM = pl.BlockSpec(memory_space=pltpu.HBM)


def iota(shape, dim):
    return lax.broadcasted_iota(jnp.int32, shape, dim)


def kept(z):
    return (z + 1) // 2 % 2


def sketch_kernel(
    away, lengths, hid_kind, hid_sign, out_kind, out_sign, hid_table, out_table, hidden, out_grad, x,
    hid_buf, out_buf, hid_tab, out_tab, counts, hid_pick, hid_neg, out_pick, out_neg, s_in, s_out, small_sems, hid_sem, out_sem,
):
    which = kept(lax.axis_index("tensor"))
    which = 1 - which if away else which
    rows, _ = hid_buf.shape
    small = [
        pltpu.make_async_copy(src, dst, small_sems.at[n])
        for n, (src, dst) in enumerate(
            [
                (out_kind, out_pick),
                (out_sign, out_neg),
                (hid_kind, hid_pick),
                (hid_sign, hid_neg),
                (out_table, out_tab),
                (hid_table, hid_tab),
                (lengths, counts),
            ]
        )
    ]
    for copy in small:
        copy.start()
    here = pl.ds(pl.multiple_of(which * rows, rows), rows)
    out_copy = pltpu.make_async_copy(out_grad.at[here], out_buf, out_sem)
    out_copy.start()
    hid_copy = pltpu.make_async_copy(hidden.at[here], hid_buf, hid_sem)
    hid_copy.start()
    _, width, size = hid_tab.shape
    for copy in small:
        copy.wait()

    def fill(pick, neg, tab, s):
        for j in range(pick.shape[0]):
            block = tab[pick[j]]
            s[:, j * size : (j + 1) * size] = jnp.where(neg[j] > 0, block, -block)

    def times(left, right):
        return lax.dot_general(left, right, (((1,), (1,)), ((), ())), preferred_element_type=F32)

    fill(out_pick, out_neg, out_tab, s_out)
    fill(hid_pick, hid_neg, hid_tab, s_in)
    out_copy.wait()
    x[width:, :] = times(s_out[...], out_buf[...])
    hid_copy.wait()
    total = times(s_in[...], hid_buf[...])
    count = counts[which]
    live = iota(total.shape, 1) < count
    scale = lax.rsqrt(jnp.full((1, total.shape[1]), count, jnp.int32).astype(F32))
    x[:width, :] = jnp.where(live, total * scale, 0.0)


def sketch(away, hidden, out_grad, lengths, hid_kind, hid_sign, hid_table, out_kind, out_sign, out_table, length):
    deep, wide = hidden.shape[1], out_grad.shape[1]
    operands = (lengths, hid_kind, hid_sign, out_kind, out_sign, hid_table, out_table, hidden, out_grad)
    return pl.pallas_call(
        functools.partial(sketch_kernel, away),
        out_shape=jax.ShapeDtypeStruct((2 * hid_table.shape[1], length), F32),
        in_specs=[HBM] * len(operands),
        out_specs=VMEM,
        scratch_shapes=[
            pltpu.VMEM((length, deep), BF16),
            pltpu.VMEM((length, wide), BF16),
            pltpu.VMEM(hid_table.shape, BF16),
            pltpu.VMEM(out_table.shape, BF16),
            pltpu.SMEM(lengths.shape, jnp.int32),
            pltpu.SMEM(hid_kind.shape, jnp.int32),
            pltpu.SMEM(hid_sign.shape, jnp.int32),
            pltpu.SMEM(out_kind.shape, jnp.int32),
            pltpu.SMEM(out_sign.shape, jnp.int32),
            pltpu.VMEM((hid_table.shape[1], deep), BF16),
            pltpu.VMEM((out_table.shape[1], wide), BF16),
            pltpu.SemaphoreType.DMA((7,)),
            pltpu.SemaphoreType.DMA,
            pltpu.SemaphoreType.DMA,
        ],
        compiler_params=pltpu.CompilerParams(vmem_limit_bytes=24 * 2**20),
        name="sketch_away" if away else "sketch_own",
    )(*[pltpu.with_memory_space_constraint(v, pltpu.HBM) for v in operands])


def split(x, parts):
    out = []
    for _ in range(parts):
        piece = x.astype(BF16)
        out.append(piece)
        x = x - piece.astype(F32)
    return out


def outer_kernel(x_ref, other, feats):
    x = x_ref[...] + other[...]
    width = x.shape[0] // 2
    a = jnp.concatenate(split(x[:width], 2), axis=0)
    b = jnp.concatenate(split(x[width:], 2), axis=0)
    z = lax.dot_general(b, a, (((1,), (1,)), ((), ())), preferred_element_type=F32)
    z = z[:width] + z[width:]
    spread = (iota((2 * width, LANES), 0) % width == iota((2 * width, LANES), 1) // 4).astype(BF16)
    y = jnp.dot(jnp.concatenate(split(z, 3), axis=0), spread, preferred_element_type=F32)
    y = y[:width] + y[width : 2 * width] + y[2 * width :]
    own = iota((SUB, LANES), 1) % 4
    total = jnp.zeros((SUB, LANES), F32)
    for q in range(4):
        total += jnp.where(own == q, y[q * SUB : (q + 1) * SUB], 0.0)
    for n in range(feats.shape[0]):
        feats[n] = total


def outer(x, other, takers):
    return pl.pallas_call(
        outer_kernel,
        out_shape=jax.ShapeDtypeStruct((takers, SUB, LANES), F32),
        in_specs=[VMEM, VMEM],
        out_specs=VMEM,
        compiler_params=pltpu.CompilerParams(vmem_limit_bytes=8 * 2**20),
        name="outer",
    )(x, other)


def whiten_kernel(ridge, gathered, out, aug, across, prods, ridge_here, sem):
    copy = pltpu.make_async_copy(ridge, ridge_here, sem)
    copy.start()
    seqs = gathered.shape[0]
    groups = seqs // SUB
    last = seqs // 2 - 1
    own = lax.axis_index("dp")
    for i in range(seqs):
        aug[i, seqs : seqs + SUB, :] = gathered[i]
    for h in range(2):
        aug[2 * own + h, seqs : seqs + SUB, :] = gathered[2 * last + h]
        aug[2 * last + h, seqs : seqs + SUB, :] = gathered[2 * own + h]
    for f in range(SUB):
        for j8 in range(groups):
            across[f, j8 * SUB : (j8 + 1) * SUB, :] = jnp.concatenate([aug[j8 * SUB + i, seqs + f : seqs + f + 1, :] for i in range(SUB)], axis=0)
    for f in range(SUB):
        aug[seqs + f, seqs : seqs + SUB, :] = jnp.zeros((SUB, LANES), F32)

    for i8 in range(groups):
        for i0 in range(0, SUB, 4):
            heads = [
                [jnp.broadcast_to(aug[i8 * SUB + ii, seqs + f : seqs + f + 1, :], (SUB, LANES)) for f in range(SUB)]
                for ii in range(i0, i0 + 4)
            ]
            for j8 in range(i8, groups):
                rows = [across[f, j8 * SUB : (j8 + 1) * SUB, :] for f in range(SUB)]
                for ii in range(4):
                    t = [heads[ii][f] * rows[f] for f in range(SUB)]
                    prods[i8 * SUB + i0 + ii, j8 * SUB : (j8 + 1) * SUB, :] = ((t[0] + t[1]) + (t[2] + t[3])) + (
                        (t[4] + t[5]) + (t[6] + t[7])
                    )
    before = (iota((LANES, LANES), 0) < iota((LANES, LANES), 1)).astype(BF16)
    for i8 in range(groups):
        wide = seqs - i8 * SUB
        block = prods[i8 * SUB : (i8 + 1) * SUB, i8 * SUB : seqs, :].reshape(SUB * wide, LANES)
        total = sum(jnp.dot(piece, before, preferred_element_type=F32) for piece in split(block, 2))
        aug[i8 * SUB : (i8 + 1) * SUB, i8 * SUB : seqs, :] = total.reshape(SUB, wide, LANES)
    copy.wait()
    r = ridge_here[0]
    sub = iota((SUB, LANES), 0)
    for i8 in range(groups):
        for ii in range(SUB):
            i = i8 * SUB + ii
            aug[i, i8 * SUB : (i8 + 1) * SUB, :] += jnp.where(sub == ii, r, 0.0)

    def panel(p):
        base = p * SUB
        diag = [aug[base + k, base : base + SUB, :] for k in range(SUB)]
        inv = []
        for k in range(SUB):
            inv.append(lax.rsqrt(diag[k][k : k + 1]))
            diag[k] = diag[k] * inv[k]
            for i in range(k + 1, SUB):
                diag[i] = diag[i] - diag[k][i : i + 1] * diag[k]
        for k in range(SUB):
            aug[base + k, base : base + SUB, :] = diag[k]
        for j8 in range(p + 1, groups + 1):
            rows = [aug[base + k, j8 * SUB : (j8 + 1) * SUB, :] for k in range(SUB)]
            for k in range(SUB):
                rows[k] = rows[k] * inv[k]
                for i in range(k + 1, SUB):
                    rows[i] = rows[i] - diag[k][i : i + 1] * rows[k]
            for k in range(SUB):
                aug[base + k, j8 * SUB : (j8 + 1) * SUB, :] = rows[k]

    def trail(p, i8):
        base = p * SUB
        for i0 in range(0, SUB, 4):
            heads = [
                [jnp.broadcast_to(aug[base + k, i8 * SUB + ii : i8 * SUB + ii + 1, :], (SUB, LANES)) for k in range(SUB)]
                for ii in range(i0, i0 + 4)
            ]
            for j8 in range(i8, groups + 1):
                rows = [aug[base + k, j8 * SUB : (j8 + 1) * SUB, :] for k in range(SUB)]
                for ii in range(4):
                    h = heads[ii]
                    i = i8 * SUB + i0 + ii
                    acc = aug[i, j8 * SUB : (j8 + 1) * SUB, :]
                    t = [h[k] * rows[k] for k in range(SUB)]
                    acc = acc - (((t[0] + t[1]) + (t[2] + t[3])) + ((t[4] + t[5]) + (t[6] + t[7])))
                    aug[i, j8 * SUB : (j8 + 1) * SUB, :] = acc

    panel(0)
    for p in range(groups):
        trail(p, p + 1)
        if p + 1 < groups:
            panel(p + 1)
        for i8 in range(p + 2, groups + 1):
            trail(p, i8)

    end = seqs - 1
    sol_end = aug[end, seqs : seqs + SUB, :] / aug[end, end : end + 1, :]
    sol = (aug[end - 1, seqs : seqs + SUB, :] - aug[end - 1, end : end + 1, :] * sol_end) / aug[
        end - 1, end - 1 : end, :
    ]
    x = [sol * r, sol_end * r]
    schur = [jnp.where(sub == f, r, 0.0) - r * aug[seqs + f, seqs : seqs + SUB, :] for f in range(SUB)]
    w = [jnp.zeros((SUB, LANES), F32) for _ in range(2)]
    for f in range(SUB):
        scale = lax.rsqrt(schur[f][f : f + 1])
        line = schur[f] * scale
        for i in range(f + 1, SUB):
            schur[i] = schur[i] - line[i : i + 1] * line
        for h in range(2):
            value = x[h][f : f + 1] * scale
            w[h] = jnp.where(sub == f, value, w[h])
            x[h] = x[h] - line * value
    size = SUB * LANES
    w = jnp.concatenate(w, axis=0) * jnp.sqrt(jnp.full((2 * SUB, LANES), size, F32))
    spread = (iota((LANES, size), 0) == iota((LANES, size), 1) // SUB).astype(BF16)
    wide = sum(jnp.dot(piece, spread, preferred_element_type=F32) for piece in split(w, 3))
    wide = jnp.where(iota((2 * SUB, size), 1) % SUB == iota((2 * SUB, size), 0) % SUB, wide, 0.0)
    lines = [jnp.sum(wide[h * SUB : (h + 1) * SUB], axis=0, keepdims=True) for h in range(2)]
    swap = kept(lax.axis_index("tensor") // 2 * 2) > 0
    out[0:1, :] = jnp.where(swap, lines[1], lines[0])
    out[1:2, :] = jnp.where(swap, lines[0], lines[1])


def whiten(ridge, gathered):
    seqs = gathered.shape[0]
    return pl.pallas_call(
        whiten_kernel,
        out_shape=jax.ShapeDtypeStruct((2, SUB * LANES), F32),
        in_specs=[HBM, VMEM],
        out_specs=VMEM,
        scratch_shapes=[
            pltpu.VMEM((seqs + SUB, seqs + SUB, LANES), F32),
            pltpu.VMEM((SUB, seqs, LANES), F32),
            pltpu.VMEM((seqs, seqs, LANES), F32),
            pltpu.SMEM(ridge.shape, F32),
            pltpu.SemaphoreType.DMA,
        ],
        compiler_params=pltpu.CompilerParams(vmem_limit_bytes=24 * 2**20),
        name="whiten",
    )(ridge, gathered)


def per_device(
    dp, tensor,
    hidden, out_grad, lengths, hid_kind, hid_sign, hid_table, out_kind, out_sign, out_table, ridge
):
    length = hidden.shape[0] // lengths.shape[0]

    def of(away):
        return sketch(
            away, hidden, out_grad, lengths, hid_kind, hid_sign, hid_table.swapaxes(1, 2),
            out_kind, out_sign, out_table.swapaxes(1, 2), length,
        )

    def swap(x, other):
        return lax.ppermute(x, "tensor", [(i, other(i) % tensor) for i in range(tensor)])

    x = of(True)
    x = of(False) + swap(x, lambda i: i ^ 1)
    x = x + swap(x, lambda i: i + 1 if i % 2 else i - 1)
    feats = outer(x, swap(x, lambda i: i - 3 if i % 2 else i + 3), 2 * dp)
    groups = [[d * tensor + z + h for d in range(dp) for h in range(2)] for z in range(0, tensor, 2)]
    gathered = lax.all_to_all(feats, ("dp", "tensor"), 0, 0, axis_index_groups=groups)
    return whiten(ridge, gathered)


def solution(mesh):
    return jax.shard_map(
        functools.partial(per_device, mesh.shape["dp"], mesh.shape["tensor"]),
        mesh=mesh,
        in_specs=(
            P("dp", "tensor"),
            P("dp", "tensor"),
            P("dp"),
            P("tensor"),
            P("tensor"),
            P(),
            P("tensor"),
            P("tensor"),
            P(),
            P(),
        ),
        out_specs=P("dp", None),
        check_vma=False,
    )
```
